256 devices in a mesh: blk: 64 (over y, z, x_lo), feat: 4 (over x_hi, core).
Axes of the slice: x: 4 (x_hi: 2, x_lo: 2; x = x_hi * 2 + x_lo), y: 4, z: 8, core: 2. Of those that a mesh axis runs over, the one named last changes fastest.
Arguments:
- image: bfloat16 [11264, 1152], P('blk', 'feat'), may hold values from -6 to 6
- text: bfloat16 [11264, 1152], P('blk', 'feat'), may hold values from -6 to 6
- scale: float32 [], replicated, may hold values from 0.05 to 0.12
- bias: float32 [], replicated, may hold values from -7 to -4
Outputs:
- image_grad: float32 [11264, 1152], P('blk', 'feat')
- text_grad: float32 [11264, 1152], P('blk', 'feat')
The draws below stay inside these ranges and needn't reach their ends.
All inputs are finite; a program needn't handle non-finite values.
Results may differ from the reference program's by a relative error of at most 0.0013.
Values may be sent and summed in bfloat16 or wider, within the bound.
No kernel may reach another device: no remote copies, remote signals or barrier semaphores. Data moves between devices by JAX's collectives and lax.ppermute only.
A program may use at most 64 MiB of HBM per device.

```python
import math
import jax
import jax.numpy as jnp
from jax import lax

D = 1152
B_DEV = 176
BATCH = 11264
N_BLK = 64


def steps_of(own_key, shape, cuts, low, high):
    level, own = 1.0, jax.random.fold_in(own_key, 6)
    for position, parts in cuts:
        heights = jnp.exp(jax.random.uniform(jax.random.fold_in(own, position), (parts,), jnp.float32, low / len(cuts), high / len(cuts)))
        level = level * jnp.repeat(heights, shape[position] // parts).reshape([-1 if axis == position else 1 for axis in range(len(shape))])
    return level


def centred(rng, extent, deviation, limit, pieces=(), held_as=jnp.bfloat16):
    values = jax.random.normal(rng, extent, jnp.float32) * deviation
    if len(pieces) > 0:
        values = steps_of(rng, extent, pieces, -0.22, 0.18) * values
    return jnp.clip(values, min=-limit, max=limit).astype(held_as)


def setup_inputs(seed: int = 0) -> dict:
    seeds = jax.random.split(jax.random.key(seed), 5)
    image = centred(seeds[0], (BATCH, D), 1.0, 6.0, ((0, 64), (1, 4)))
    text = centred(seeds[1], (BATCH, D), 1.0, 6.0, ((0, 64), (1, 4)))
    scale = jnp.clip(jnp.exp(jax.random.uniform(seeds[2], (), jnp.float32, math.log(0.05), math.log(0.12))), 0.05, 0.12)
    bias = jnp.clip(jax.random.uniform(seeds[3], (), jnp.float32, -7.0, -4.0), -7.0, -4.0)
    return {"image": image, "text": text, "scale": scale, "bias": bias}


def reference(image, text, scale, bias):
    total = image.shape[0]
    blocks = image.reshape(N_BLK, B_DEV, D)
    col_index = jnp.arange(total, dtype=jnp.int32)[None, :]

    def visit(carry, item):
        block_id, rows_img = item
        dots = jnp.dot(rows_img, text.T, preferred_element_type=jnp.float32)
        logit = scale * dots + bias
        row_index = block_id * B_DEV + jnp.arange(B_DEV, dtype=jnp.int32)[:, None]
        slope = jnp.where(row_index == col_index, -jax.nn.sigmoid(-logit), jax.nn.sigmoid(logit)).astype(jnp.bfloat16)
        grad_rows = scale * jnp.dot(slope, text, preferred_element_type=jnp.float32)
        carry = carry + scale * jnp.dot(slope.T, rows_img, preferred_element_type=jnp.float32)
        return carry, grad_rows

    start = jnp.zeros((total, D), jnp.float32)
    text_grad, image_parts = lax.scan(visit, start, (jnp.arange(N_BLK, dtype=jnp.int32), blocks))
    return image_parts.reshape(total, D), text_grad
```

```python
import jax
import jax.numpy as jnp
from jax import lax
from jax.experimental import pallas as pl
from jax.experimental.pallas import tpu as pltpu
from jax.sharding import Mesh
from jax.sharding import PartitionSpec as P

AXES = ("y", "z", "l", "h", "c")
SIZES = {"y": 4, "z": 8, "l": 2, "h": 2, "c": 2}
ROWS = 88
SLOT = 96
QUART = 288
HALF = 576
WIDE = 640
F32 = jnp.float32
BF16 = jnp.bfloat16
F16 = jnp.float16
VMEM = pl.BlockSpec(memory_space=pltpu.VMEM)
SMEM = pl.BlockSpec(memory_space=pltpu.SMEM)


def shape(dims, dtype):
    return jax.ShapeDtypeStruct(dims, dtype)


def call(kernel, outs, *args, smem=0, scratch=(), flops=0, mib=32):
    specs = [VMEM] * (len(args) - smem) + [SMEM] * smem
    moved = sum(a.size * a.dtype.itemsize for a in (*args, *outs))
    return pl.pallas_call(
        kernel,
        out_shape=outs,
        in_specs=specs,
        out_specs=[VMEM] * len(outs),
        scratch_shapes=list(scratch),
        compiler_params=pltpu.CompilerParams(vmem_limit_bytes=mib * 2**20),
        cost_estimate=pl.CostEstimate(flops=flops, bytes_accessed=moved, transcendentals=0),
    )(*args)


def flip(x, axis, mask):
    axes = axis if isinstance(axis, tuple) else (axis,)
    count = 1
    for a in axes:
        count *= SIZES[a]
    return lax.ppermute(x, axis, [(i, i ^ mask) for i in range(count)])


def split_kernel(image, text, image_keep, image_send, text_keep, text_send):
    for source, axis, keep, send in (
        (image, "h", image_keep, image_send),
        (text, "c", text_keep, text_send),
    ):
        low = lax.axis_index(axis) == 0
        x = source[...].astype(F32)
        first, second = x[:ROWS], x[ROWS:]
        keep[...] = jnp.where(low, first, second).astype(BF16)
        send[...] = jnp.where(low, second, first).astype(BF16)


def join_kernel(keep, recv, piece):
    joined = jnp.concatenate(
        [keep[...].astype(F32), recv[...].astype(F32), jnp.zeros((ROWS, WIDE - HALF), F32)], axis=1
    )
    piece[...] = jnp.concatenate([joined, jnp.zeros((SLOT - ROWS, WIDE), F32)], axis=0).astype(BF16)


def scaled(x):
    most = jnp.max(jnp.max(jnp.abs(x), axis=0, keepdims=True), axis=1, keepdims=True)
    power = jnp.floor(jnp.log2(jnp.maximum(most, 1e-30)))
    lane = lax.broadcasted_iota(jnp.int32, x.shape, 1)
    return jnp.where(lane < HALF, x * jnp.exp2(13.0 - power), power)


def unscaled(p):
    return p * jnp.exp2(p[:1, HALF : HALF + 1] - 13.0)


def pair_kernel(*refs):
    image_own, image_swap, text = refs[0:4], refs[4:8], refs[8:12]
    scale_ref, bias_ref = refs[12:14]
    keep, send, text_own = refs[14:17]
    text_out = refs[17:20]
    images, texts, slope, text_sum = refs[20:24]
    scale, bias = scale_ref[0], bias_ref[0]
    zeros = jnp.zeros((SLOT, WIDE - HALF), BF16)
    for k in range(4):
        for p in range(2):
            rows = pl.ds(SLOT * (2 * k + p), SLOT)
            images[rows, 0:WIDE] = image_own[k][p]
            images[rows, WIDE:] = image_swap[k][p]
            a, b = text[k][2 * p], text[k][2 * p + 1]
            texts[rows, 0:WIDE] = jnp.concatenate([a[:, :QUART], b[:, :QUART], zeros], axis=1)
            texts[rows, WIDE:] = jnp.concatenate([a[:, QUART:HALF], b[:, QUART:HALF], zeros], axis=1)
    own = lax.axis_index("h") == lax.axis_index("c")
    for j in range(3):
        cols = pl.ds(256 * j, 256)
        dots = lax.dot_general(
            images[...], texts[cols, :], (((1,), (1,)), ((), ())), preferred_element_type=F32
        )
        logit = scale * dots + bias
        if j == 0:
            row = lax.broadcasted_iota(jnp.int32, logit.shape, 0)
            col = lax.broadcasted_iota(jnp.int32, logit.shape, 1)
            paired = (row == col) & (row < ROWS) & own
            value = jnp.where(paired, -jax.nn.sigmoid(-logit), jax.nn.sigmoid(logit))
        else:
            value = jax.nn.sigmoid(logit)
        value = value.astype(BF16)
        slope[:, cols] = value
        text_sum[cols, :] = lax.dot_general(
            value, images[...], (((0,), (0,)), ((), ())), preferred_element_type=F32
        )
    add = jnp.dot(slope[...], texts[...], preferred_element_type=F32)
    for s in range(8):
        keep[s] = add[SLOT * s : SLOT * (s + 1), :WIDE]
        send[s] = add[SLOT * s : SLOT * (s + 1), WIDE:]
    pad = jnp.zeros((SLOT, WIDE - HALF), F32)
    for e in range(4):
        parts = []
        for p in range(2):
            x = text_sum[pl.ds(SLOT * (2 * e + p), SLOT), :]
            for d in range(2):
                low, high = x[:, QUART * d : QUART * (d + 1)], x[:, WIDE + QUART * d : WIDE + QUART * (d + 1)]
                parts.append(jnp.concatenate([low, high, pad], axis=1))
        if e == 0:
            for n in range(4):
                text_own[n] = parts[n]
        else:
            for n in range(4):
                text_out[e - 1][n] = scaled(parts[n])


def image_first_kernel(keep, recv, own, *outs):
    for s in range(8):
        x = keep[s] + recv[s]
        if s < 2:
            own[s] = x
        else:
            outs[s // 2 - 1][s % 2] = scaled(x)


def text_second_kernel(own, r1, r2, r3, kept, *outs):
    for n in range(4):
        x = own[n] + unscaled(r1[n]) + unscaled(r2[n]) + unscaled(r3[n])
        if n == 0:
            kept[...] = x
        else:
            outs[n - 1][...] = scaled(x)


def image_second_kernel(own, r1, r2, r3, kept, out):
    for n in range(2):
        x = own[n] + unscaled(r1[n]) + unscaled(r2[n]) + unscaled(r3[n])
        if n == 0:
            kept[...] = x
        else:
            out[...] = scaled(x)


def last_kernel(*refs):
    *parts, scale, keep, send = refs
    x = parts[0][...]
    for part in parts[1:]:
        x = x + unscaled(part[...])
    x = scale[0] * x[:ROWS]
    keep[...] = x[:, :QUART]
    send[...] = x[:, QUART:HALF]


def place_kernel(image_keep, image_recv, text_keep, text_recv, image_out, text_out):
    for axis, keep, recv, out in (
        ("h", image_keep, image_recv, image_out),
        ("c", text_keep, text_recv, text_out),
    ):
        low = lax.axis_index(axis) == 0
        a, b = keep[...], recv[...]
        out[:ROWS] = jnp.where(low, a, b)
        out[ROWS:] = jnp.where(low, b, a)


def shards(image, text, scale, bias):
    scale, bias = scale.reshape(1), bias.reshape(1)
    half = shape((ROWS, QUART), BF16)
    image_keep, image_send, text_keep, text_send = call(split_kernel, [half] * 4, image, text)
    image_recv = flip(image_send, "h", 1)
    text_recv = flip(text_send, "c", 1)
    piece = [shape((SLOT, WIDE), BF16)]
    (text_piece,) = call(join_kernel, piece, text_keep, text_recv)
    (image_piece,) = call(join_kernel, piece, image_keep, image_recv)

    x_axes = ("l", "h")
    texts = jnp.stack([text_piece] + [flip(text_piece, x_axes, n) for n in (1, 2, 3)])
    images = jnp.stack([image_piece, flip(image_piece, "z", 1)])
    text_all = [texts] + [flip(texts, "y", n) for n in (1, 2, 3)]
    image_all = [images] + [flip(images, "z", n) for n in (2, 4, 6)]
    image_swap = [flip(x, "c", 1) for x in image_all]

    big = shape((8, SLOT, WIDE), F32)
    four, two, one = (shape((*d, SLOT, WIDE), F32) for d in ((4,), (2,), ()))
    keep, send, text_own, *text_out = call(
        pair_kernel,
        [big, big, four, four, four, four],
        *image_all,
        *image_swap,
        *text_all,
        scale,
        bias,
        smem=2,
        scratch=[
            pltpu.VMEM((8 * SLOT, 2 * WIDE), BF16),
            pltpu.VMEM((8 * SLOT, 2 * WIDE), BF16),
            pltpu.VMEM((8 * SLOT, 8 * SLOT), BF16),
            pltpu.VMEM((8 * SLOT, 2 * WIDE), F32),
        ],
        flops=6 * 704 * 704 * 1152,
        mib=56,
    )

    def across(x, axis, mask):
        return flip(x.astype(F16), axis, mask).astype(F32)

    recv = flip(send, "c", 1)
    text_in = [across(x, "y", n) for n, x in zip((1, 2, 3), text_out)]
    image_own, *image_out = call(image_first_kernel, [two] * 4, keep, recv)
    image_in = [across(x, "z", n) for n, x in zip((2, 4, 6), image_out)]
    text_own, *text_out = call(text_second_kernel, [one] * 4, text_own, *text_in)
    text_in = [across(x, x_axes, n) for n, x in zip((1, 2, 3), text_out)]
    image_own, image_out = call(image_second_kernel, [one] * 2, image_own, *image_in)
    image_in = across(image_out, "z", 1)
    part = [shape((ROWS, QUART), F32)] * 2
    image_keep, image_send = call(last_kernel, part, image_own, image_in, scale, smem=1)
    image_recv = flip(image_send, "h", 1)
    text_keep, text_send = call(last_kernel, part, text_own, *text_in, scale, smem=1)
    text_recv = flip(text_send, "c", 1)
    grads = [shape((2 * ROWS, QUART), F32)] * 2
    return tuple(call(place_kernel, grads, image_keep, image_recv, text_keep, text_recv))


def solution(mesh):
    fine = Mesh(mesh.devices.reshape([SIZES[a] for a in AXES]), AXES)
    spec = P(("y", "z", "l"), ("h", "c"))
    return jax.shard_map(
        shards, mesh=fine, in_specs=(spec, spec, P(), P()), out_specs=(spec, spec), check_vma=False
    )
```

```python
import jax
import jax.numpy as jnp
from jax import lax
from jax.experimental import pallas as pl
from jax.experimental.pallas import tpu as pltpu
from jax.sharding import Mesh
from jax.sharding import PartitionSpec as P

AXES = ("y", "z", "l", "h", "c")
SIZES = {"y": 4, "z": 8, "l": 2, "h": 2, "c": 2}
ROWS = 88
SLOT = 96
CUT = 48
FAR = 240
QUART = 288
HALF = 576
WIDE = 640
X = ("l", "h")
F32 = jnp.float32
BF16 = jnp.bfloat16
F16 = jnp.float16
VMEM = pl.BlockSpec(memory_space=pltpu.VMEM)
SMEM = pl.BlockSpec(memory_space=pltpu.SMEM)


def shape(dims, dtype):
    return jax.ShapeDtypeStruct(dims, dtype)


def call(kernel, outs, *args, smem=0, scratch=(), flops=0, mib=32):
    specs = [VMEM] * (len(args) - smem) + [SMEM] * smem
    moved = sum(a.size * a.dtype.itemsize for a in (*args, *outs))
    return pl.pallas_call(
        kernel,
        out_shape=outs,
        in_specs=specs,
        out_specs=[VMEM] * len(outs),
        scratch_shapes=list(scratch),
        compiler_params=pltpu.CompilerParams(vmem_limit_bytes=mib * 2**20),
        cost_estimate=pl.CostEstimate(flops=flops, bytes_accessed=moved, transcendentals=0),
    )(*args)


def flip(x, axis, mask):
    count = 4 if axis == X else SIZES[axis]
    return lax.ppermute(x, axis, [(i, i ^ mask) for i in range(count)])


def behind(x, axis, distance):
    count = SIZES[axis]
    return lax.ppermute(x, axis, [(i, (i + distance) % count) for i in range(count)])


def together(*xs):
    return lax.optimization_barrier(xs)


def split_kernel(image, text, image_keep, image_send, text_keep, text_send):
    for source, axis, keep, send in (
        (image, "h", image_keep, image_send),
        (text, "c", text_keep, text_send),
    ):
        low = lax.axis_index(axis) == 0
        x = source[...].astype(F32)
        first, second = x[:ROWS], x[ROWS:]
        keep[...] = jnp.where(low, first, second).astype(BF16)
        send[...] = jnp.where(low, second, first).astype(BF16)


def joined(a, b):
    x = jnp.concatenate([a, b, jnp.zeros((ROWS, WIDE - HALF), F32)], axis=1)
    return jnp.concatenate([x, jnp.zeros((SLOT - ROWS, WIDE), F32)], axis=0).astype(BF16)


def piece_kernel(keep, recv, out):
    out[...] = joined(keep[...].astype(F32), recv[...].astype(F32))


def stack_kernel(*refs):
    for n, ref in enumerate(refs[:-1]):
        refs[-1][n] = ref[...]


def image_near_kernel(own, below, above, near, up, down):
    x, a, b = own[...], below[...], above[...]
    for out, parts in ((near, (x, a, b)), (up, (x, b, a[:CUT])), (down, (x, a, b[CUT:]))):
        for n, part in enumerate(parts):
            out[pl.ds(SLOT * n, part.shape[0]), :] = part


def scaled(x):
    most = jnp.max(jnp.max(jnp.abs(x), axis=0, keepdims=True), axis=1, keepdims=True)
    power = jnp.floor(jnp.log2(jnp.maximum(most, 1e-30)))
    lane = lax.broadcasted_iota(jnp.int32, x.shape, 1)
    return jnp.where(lane < HALF, x * jnp.exp2(13.0 - power), power)


def unscaled(p):
    return p * jnp.exp2(p[:1, HALF : HALF + 1] - 13.0)


def slope_kernel(*refs):
    halves, text = (refs[0:3], refs[3:6]), refs[6:10]
    scale_ref, bias_ref = refs[10:12]
    keep, send, slope, images = refs[12:16]
    texts = refs[16]
    scale, bias = scale_ref[0], bias_ref[0]
    zeros = jnp.zeros((SLOT, WIDE - HALF), BF16)
    for c, (near, below, above) in enumerate(halves):
        lanes = pl.ds(WIDE * c, WIDE)
        for first, source, count in (
            (0, near, 3 * SLOT),
            (3 * SLOT, below, 2 * SLOT),
            (5 * SLOT, above, 2 * SLOT),
        ):
            images[pl.ds(first, count), lanes] = source[:count, :]
        images[pl.ds(7 * SLOT, CUT), lanes] = below[2 * SLOT :, :]
        images[pl.ds(7 * SLOT + CUT, CUT), lanes] = above[2 * SLOT :, :]
    for s in range(8):
        rows = pl.ds(SLOT * s, SLOT)
        a, b = text[s // 4 * 2][s % 4], text[s // 4 * 2 + 1][s % 4]
        texts[rows, 0:WIDE] = jnp.concatenate([a[:, :QUART], b[:, :QUART], zeros], axis=1)
        texts[rows, WIDE:] = jnp.concatenate([a[:, QUART:HALF], b[:, QUART:HALF], zeros], axis=1)
    own = lax.axis_index("h") == lax.axis_index("c")
    for j in range(3):
        cols = pl.ds(256 * j, 256)
        dots = lax.dot_general(
            images[...], texts[cols, :], (((1,), (1,)), ((), ())), preferred_element_type=F32
        )
        logit = scale * dots + bias
        value = jax.nn.sigmoid(logit)
        if j == 0:
            top = logit[:SLOT]
            row = lax.broadcasted_iota(jnp.int32, top.shape, 0)
            col = lax.broadcasted_iota(jnp.int32, top.shape, 1)
            paired = (col == row) & (row < ROWS) & own
            top = jnp.where(paired, -jax.nn.sigmoid(-top), value[:SLOT])
            value = jnp.concatenate([top, value[SLOT:]], axis=0)
        slope[:, cols] = value.astype(BF16)
    add = jnp.dot(slope[...], texts[...], preferred_element_type=F32)
    for s in range(8):
        keep[s] = add[SLOT * s : SLOT * (s + 1), :WIDE]
        send[s] = add[SLOT * s : SLOT * (s + 1), WIDE:]


def text_kernel(slope, images, own, *outs):
    total = lax.dot_general(
        slope[...], images[...], (((0,), (0,)), ((), ())), preferred_element_type=F32
    )
    pad = jnp.zeros((SLOT, WIDE - HALF), F32)
    for s in range(8):
        x = total[SLOT * s : SLOT * (s + 1), :]
        for d in range(2):
            low, high = x[:, QUART * d : QUART * (d + 1)], x[:, WIDE + QUART * d : WIDE + QUART * (d + 1)]
            part = jnp.concatenate([low, high, pad], axis=1)
            m = s // 4 * 2 + d
            if m == 0:
                own[s % 4] = part
            else:
                outs[m - 1][s % 4] = scaled(part)


def image_first_kernel(keep, recv, own, below, above):
    for s in range(8):
        x = keep[s] + recv[s]
        if s < 3:
            own[s] = x
        elif s < 7:
            out = below if s < 5 else above
            out[pl.ds(SLOT * ((s - 3) % 2), SLOT), :] = scaled(x)
        else:
            x = scaled(x)
            below[pl.ds(2 * SLOT, CUT), :] = x[:CUT]
            above[pl.ds(2 * SLOT, CUT), :] = x[CUT:]


def image_sum_kernel(own, from_above, from_below, kept, below, above):
    a = [unscaled(from_above[n * SLOT : min((n + 1) * SLOT, FAR), :]) for n in range(3)]
    b = [unscaled(from_below[n * SLOT : min((n + 1) * SLOT, FAR), :]) for n in range(3)]
    kept[...] = own[0] + a[0] + b[0]
    x = own[1] + b[1]
    below[...] = scaled(jnp.concatenate([x[:CUT] + a[2], x[CUT:]], axis=0))
    x = own[2] + a[1]
    above[...] = scaled(jnp.concatenate([x[:CUT], x[CUT:] + b[2]], axis=0))


def text_sum_kernel(own, r1, r2, r3, kept, *outs):
    for n in range(4):
        x = own[n] + unscaled(r1[n]) + unscaled(r2[n]) + unscaled(r3[n])
        if n == 0:
            kept[...] = x
        else:
            outs[n - 1][...] = scaled(x)


def last_kernel(*refs):
    own, *parts, scale, keep, send = refs
    x = own[...]
    for part in parts:
        x = x + unscaled(part[...])
    x = scale[0] * x[:ROWS]
    keep[...] = x[:, :QUART]
    send[...] = x[:, QUART:HALF]


def place_kernel(image_keep, image_recv, text_keep, text_recv, image_out, text_out):
    for axis, keep, recv, out in (
        ("h", image_keep, image_recv, image_out),
        ("c", text_keep, text_recv, text_out),
    ):
        low = lax.axis_index(axis) == 0
        a, b = keep[...], recv[...]
        out[:ROWS] = jnp.where(low, a, b)
        out[ROWS:] = jnp.where(low, b, a)


def shards(image, text, scale, bias):
    scale, bias = scale.reshape(1), bias.reshape(1)
    half = shape((ROWS, QUART), BF16)
    image_keep, image_send, text_keep, text_send = call(split_kernel, [half] * 4, image, text, mib=4)
    text_recv = flip(text_send, "c", 1)
    piece = [shape((SLOT, WIDE), BF16)]
    (text,) = call(piece_kernel, piece, text_keep, text_recv, mib=4)

    four = [text] + [flip(text, "y", n) for n in (1, 2, 3)]
    image_recv = flip(image_send, "h", 1)
    (image,) = call(piece_kernel, piece, image_keep, image_recv, mib=4)
    (four,) = call(stack_kernel, [shape((4, SLOT, WIDE), BF16)], *four, mib=4)
    four, image = together(four, image)
    texts = [four] + [flip(four, X, n) for n in (1, 2, 3)]
    near, up, down = call(
        image_near_kernel,
        [shape((n, WIDE), BF16) for n in (3 * SLOT, FAR, FAR)],
        image,
        behind(image, "z", 3),
        behind(image, "z", -3),
        mib=4,
    )
    images = [near, behind(up, "z", 1), behind(down, "z", -1)]
    *images, t0, t1, t2, t3 = together(*images, *texts)
    texts = [t0, t1, t2, t3]
    swapped = [flip(x, "c", 1) for x in images]

    big, quad, three, one = (shape((*d, SLOT, WIDE), F32) for d in ((8,), (4,), (3,), ()))
    far = shape((FAR, WIDE), F32)
    keep, send, slope, images = call(
        slope_kernel,
        [big, big, shape((8 * SLOT, 8 * SLOT), BF16), shape((8 * SLOT, 2 * WIDE), BF16)],
        *images,
        *swapped,
        *texts,
        scale,
        bias,
        smem=2,
        scratch=[pltpu.VMEM((8 * SLOT, 2 * WIDE), BF16)],
        flops=4 * 704 * 704 * 1152,
        mib=16,
    )
    recv = flip(send, "c", 1)
    text_own, *text_out = call(text_kernel, [quad] * 4, slope, images, flops=2 * 704 * 704 * 1152, mib=12)
    image_own, below, above = call(image_first_kernel, [three, far, far], keep, recv, mib=12)
    below, above, *text_out = together(below, above, *text_out)

    def across(x, move, axis, n):
        return move(x.astype(F16), axis, n).astype(F32)

    text_in = [across(x, flip, X, n) for n, x in enumerate(text_out, 1)]
    image_in = [across(below, behind, "z", -1), across(above, behind, "z", 1)]
    image_own, below, above = call(image_sum_kernel, [one] * 3, image_own, *image_in, mib=8)
    below, above = across(below, behind, "z", -3), across(above, behind, "z", 3)
    below, above, *text_in = together(below, above, *text_in)
    text_own, *text_out = call(text_sum_kernel, [one] * 4, text_own, *text_in, mib=12)
    text_in = [across(x, flip, "y", n) for n, x in enumerate(text_out, 1)]
    image_in = [below, above]
    part = [shape((ROWS, QUART), F32)] * 2
    image_keep, image_send = call(last_kernel, part, image_own, *image_in, scale, smem=1, mib=4)
    image_recv = flip(image_send, "h", 1)
    text_keep, text_send = call(last_kernel, part, text_own, *text_in, scale, smem=1, mib=4)
    text_recv = flip(text_send, "c", 1)
    grads = [shape((2 * ROWS, QUART), F32)] * 2
    return tuple(call(place_kernel, grads, image_keep, image_recv, text_keep, text_recv, mib=4))


def solution(mesh):
    fine = Mesh(mesh.devices.reshape([SIZES[a] for a in AXES]), AXES)
    spec = P(("y", "z", "l"), ("h", "c"))
    return jax.shard_map(
        shards, mesh=fine, in_specs=(spec, spec, P(), P()), out_specs=(spec, spec), check_vma=False
    )
```

```python
import jax
import jax.numpy as jnp
from jax import lax
from jax.experimental import pallas as pl
from jax.experimental.pallas import tpu as pltpu
from jax.sharding import Mesh
from jax.sharding import PartitionSpec as P

AXES = ("y", "z", "l", "h", "c")
SIZES = {"y": 4, "z": 8, "l": 2, "h": 2, "c": 2}
ROWS = 88
SLOT = 96
QUART = 288
HALF = 576
WIDE = 640
X = ("l", "h")
F32 = jnp.float32
BF16 = jnp.bfloat16
F16 = jnp.float16
VMEM = pl.BlockSpec(memory_space=pltpu.VMEM)
SMEM = pl.BlockSpec(memory_space=pltpu.SMEM)


def shape(dims, dtype):
    return jax.ShapeDtypeStruct(dims, dtype)


def call(kernel, outs, *args, smem=0, scratch=(), flops=0, mib=32):
    specs = [VMEM] * (len(args) - smem) + [SMEM] * smem
    moved = sum(a.size * a.dtype.itemsize for a in (*args, *outs))
    return pl.pallas_call(
        kernel,
        out_shape=outs,
        in_specs=specs,
        out_specs=[VMEM] * len(outs),
        scratch_shapes=list(scratch),
        compiler_params=pltpu.CompilerParams(vmem_limit_bytes=mib * 2**20),
        cost_estimate=pl.CostEstimate(flops=flops, bytes_accessed=moved, transcendentals=0),
    )(*args)


def flip(x, axis, mask):
    count = 4 if axis == X else SIZES[axis]
    return lax.ppermute(x, axis, [(i, i ^ mask) for i in range(count)])


def behind(x, axis, distance):
    count = SIZES[axis]
    return lax.ppermute(x, axis, [(i, (i + distance) % count) for i in range(count)])


def together(*xs):
    return lax.optimization_barrier(xs)


def split_kernel(image, text, image_keep, image_send, text_keep, text_send):
    for source, axis, keep, send in (
        (image, "h", image_keep, image_send),
        (text, "c", text_keep, text_send),
    ):
        low = lax.axis_index(axis) == 0
        x = source[...].astype(F32)
        first, second = x[:ROWS], x[ROWS:]
        keep[...] = jnp.where(low, first, second).astype(BF16)
        sent = jnp.where(low, second, first)
        if send is image_send:
            sent = jnp.concatenate([sent, jnp.zeros((ROWS, WIDE - QUART), F32)], axis=1)
            sent = jnp.concatenate([sent, jnp.zeros((SLOT - ROWS, WIDE), F32)], axis=0)
        send[...] = sent.astype(BF16)


def piece_kernel(keep, recv, out):
    a, b = keep[...].astype(F32), recv[...].astype(F32)[:ROWS, :QUART]
    out[...] = jnp.concatenate([a, b, jnp.zeros((ROWS, WIDE - HALF), F32)], axis=1).astype(BF16)


def stack_kernel(*refs):
    for n, ref in enumerate(refs[:-1]):
        refs[-1][n] = ref[...]


def scaled(x):
    most = jnp.max(jnp.max(jnp.abs(x), axis=0, keepdims=True), axis=1, keepdims=True)
    power = jnp.floor(jnp.log2(jnp.maximum(most, 1e-30)))
    lane = lax.broadcasted_iota(jnp.int32, x.shape, 1)
    return jnp.where(lane < HALF, x * jnp.exp2(13.0 - power), power)


def unscaled(p):
    return p * jnp.exp2(p[:1, HALF : HALF + 1] - 13.0)


def slope_kernel(*refs):
    halves, text, across = (refs[0:3], refs[3:6]), refs[6:9], refs[9:13]
    scale_ref, bias_ref = refs[13:15]
    keep, send, slope, images = refs[15:19]
    texts = refs[19]
    scale, bias = scale_ref[0], bias_ref[0]
    zeros = jnp.zeros((ROWS, WIDE - HALF), BF16)
    for s in range(8):
        rows = pl.ds(SLOT * s, ROWS)
        for half, parts in enumerate(halves):
            images[rows, WIDE * half : WIDE * (half + 1)] = parts[s // 3][s % 3]
        a, b = (text[0][s], across[s][...]) if s < 4 else (text[1][s - 4], text[2][s - 4])
        texts[rows, 0:WIDE] = jnp.concatenate([a[:, :QUART], b[:, :QUART], zeros], axis=1)
        texts[rows, WIDE:] = jnp.concatenate([a[:, QUART:HALF], b[:, QUART:HALF], zeros], axis=1)
        rows = pl.ds(SLOT * s + ROWS, SLOT - ROWS)
        images[rows, :] = jnp.zeros((SLOT - ROWS, 2 * WIDE), BF16)
        texts[rows, :] = jnp.zeros((SLOT - ROWS, 2 * WIDE), BF16)
    own = lax.axis_index("h") == lax.axis_index("c")
    for j in range(3):
        cols = pl.ds(256 * j, 256)
        dots = lax.dot_general(
            images[...], texts[cols, :], (((1,), (1,)), ((), ())), preferred_element_type=F32
        )
        logit = scale * dots + bias
        value = jax.nn.sigmoid(logit)
        if j == 0:
            top = logit[:SLOT]
            row = lax.broadcasted_iota(jnp.int32, top.shape, 0)
            col = lax.broadcasted_iota(jnp.int32, top.shape, 1)
            paired = (col == row) & (row < ROWS) & own
            top = jnp.where(paired, -jax.nn.sigmoid(-top), value[:SLOT])
            value = jnp.concatenate([top, value[SLOT:]], axis=0)
        slope[:, cols] = value.astype(BF16)
    add = jnp.dot(slope[...], texts[...], preferred_element_type=F32)
    for s in range(8):
        keep[s] = add[SLOT * s : SLOT * s + ROWS, :WIDE]
        send[s] = add[SLOT * s : SLOT * s + ROWS, WIDE:]


def text_kernel(slope, images, own, two, three, *across):
    total = lax.dot_general(
        slope[...], images[...], (((0,), (0,)), ((), ())), preferred_element_type=F32
    )
    pad = jnp.zeros((ROWS, WIDE - HALF), F32)
    for s in range(8):
        x = total[SLOT * s : SLOT * s + ROWS, :]
        for d in range(2):
            low, high = x[:, QUART * d : QUART * (d + 1)], x[:, WIDE + QUART * d : WIDE + QUART * (d + 1)]
            part = jnp.concatenate([low, high, pad], axis=1)
            if s >= 4:
                (two, three)[d][s - 4] = scaled(part)
            elif d == 0:
                own[s] = part
            else:
                across[s][...] = part if s == 0 else scaled(part)


def image_first_kernel(keep, recv, own, below, above):
    for s in range(8):
        x = keep[s] + recv[s]
        if s < 3:
            own[s] = x
        else:
            (below, above)[s // 3 - 1][s % 3] = scaled(x)


def image_sum_kernel(own, from_above, from_below, kept, below, above):
    kept[...] = own[0] + unscaled(from_above[0]) + unscaled(from_below[0])
    below[...] = scaled(own[1] + unscaled(from_above[1]) + unscaled(from_below[1]))
    above[...] = scaled(own[2] + unscaled(from_above[2]))


def text_across_kernel(own, r1, r2, r3, out):
    out[...] = scaled(own[...] + unscaled(r1[...]) + unscaled(r2[...]) + unscaled(r3[...]))


def text_sum_kernel(own, r2, r3, kept, *outs):
    for n in range(4):
        x = own[n] + unscaled(r2[n]) + unscaled(r3[n])
        if n == 0:
            kept[...] = x
        else:
            outs[n - 1][...] = scaled(x)


def last_kernel(*refs):
    own, *parts, scale, keep, send = refs
    x = own[...]
    for part in parts:
        x = x + unscaled(part[...])
    x = scale[0] * x
    keep[...] = x[:, :QUART]
    send[:, :QUART] = x[:, QUART:HALF]
    send[:, QUART:] = jnp.zeros((ROWS, send.shape[1] - QUART), F32)


def place_kernel(image_keep, image_recv, text_keep, text_recv, image_out, text_out):
    for axis, keep, recv, out in (
        ("h", image_keep, image_recv, image_out),
        ("c", text_keep, text_recv, text_out),
    ):
        low = lax.axis_index(axis) == 0
        a, b = keep[...], recv[...][:, :QUART]
        out[:ROWS] = jnp.where(low, a, b)
        out[ROWS:] = jnp.where(low, b, a)


def shards(image, text, scale, bias):
    scale, bias = scale.reshape(1), bias.reshape(1)
    half = shape((ROWS, QUART), BF16)
    image_keep, image_send, text_keep, text_send = call(
        split_kernel, [half, shape((SLOT, WIDE), BF16), half, half], image, text, mib=4
    )
    image_recv = flip(image_send, "h", 1)
    text_recv = flip(text_send, "c", 1)
    piece = [shape((ROWS, WIDE), BF16)]
    (text,) = call(piece_kernel, piece, text_keep, text_recv, mib=4)
    (image,) = call(piece_kernel, piece, image_keep, image_recv, mib=4)

    def stacked(*xs):
        return call(stack_kernel, [shape((len(xs), ROWS, WIDE), BF16)], *xs, mib=4)[0]

    four = stacked(text, *(flip(text, "y", n) for n in (1, 2, 3)))
    other = flip(text, "h", 1)
    other = [other] + [flip(other, "y", n) for n in (1, 2, 3)]
    texts = [four] + [flip(four, X, n) for n in (2, 3)]
    near = image, behind(image, "z", 3), behind(image, "z", -3)
    trio, duo, *other = together(stacked(*near), stacked(*near[:2]), *other)
    images = [trio, behind(trio, "z", 1), behind(duo, "z", -1)]
    *images, t0, t1, t2 = together(*images, *texts)
    texts = [t0, t1, t2, *other]
    swapped = [flip(x, "c", 1) for x in images]

    big, quad, three, one = (shape((*d, ROWS, WIDE), F32) for d in ((8,), (4,), (3,), ()))
    two = shape((2, ROWS, WIDE), F32)
    keep, send, slope, images = call(
        slope_kernel,
        [big, big, shape((8 * SLOT, 8 * SLOT), BF16), shape((8 * SLOT, 2 * WIDE), BF16)],
        *images,
        *swapped,
        *texts,
        scale,
        bias,
        smem=2,
        scratch=[pltpu.VMEM((8 * SLOT, 2 * WIDE), BF16)],
        flops=4 * 704 * 704 * 1152,
        mib=16,
    )
    recv = flip(send, "c", 1)
    text_own, *text_out = call(
        text_kernel, [quad] * 3 + [one] * 4, slope, images, flops=2 * 704 * 704 * 1152, mib=12
    )
    text_out, text_across, *across_out = text_out[:2], *text_out[2:]
    image_own, below, above = call(image_first_kernel, [three, three, two], keep, recv, mib=12)
    below, above, *text_out = together(below, above, *text_out)

    def moved(x, move, axis, n):
        return move(x.astype(F16), axis, n).astype(F32)

    across_in = [moved(x, flip, "y", n) for n, x in enumerate(across_out, 1)]
    text_in = [moved(x, flip, X, n) for n, x in zip((2, 3), text_out)]
    image_in = [moved(below, behind, "z", -1), moved(above, behind, "z", 1)]
    (across,) = call(text_across_kernel, [one], text_across, *across_in, mib=4)
    across = moved(across, flip, "h", 1)
    image_own, below, above = call(image_sum_kernel, [one] * 3, image_own, *image_in, mib=8)
    below, above = moved(below, behind, "z", -3), moved(above, behind, "z", 3)
    below, above, *text_in = together(below, above, *text_in)
    text_own, *text_out = call(text_sum_kernel, [one] * 4, text_own, *text_in, mib=12)
    text_in = [across] + [moved(x, flip, "y", n) for n, x in enumerate(text_out, 1)]
    image_in = [below, above]
    part = [shape((ROWS, n), F32) for n in (QUART, 384)]
    image_keep, image_send = call(last_kernel, part, image_own, *image_in, scale, smem=1, mib=4)
    image_recv = flip(image_send, "h", 1)
    text_keep, text_send = call(last_kernel, part, text_own, *text_in, scale, smem=1, mib=4)
    text_recv = flip(text_send, "c", 1)
    grads = [shape((2 * ROWS, QUART), F32)] * 2
    return tuple(call(place_kernel, grads, image_keep, image_recv, text_keep, text_recv, mib=4))


def solution(mesh):
    fine = Mesh(mesh.devices.reshape([SIZES[a] for a in AXES]), AXES)
    spec = P(("y", "z", "l"), ("h", "c"))
    return jax.shard_map(
        shards, mesh=fine, in_specs=(spec, spec, P(), P()), out_specs=(spec, spec), check_vma=False
    )
```

```python
import jax
import jax.numpy as jnp
from jax import lax
from jax.experimental import pallas as pl
from jax.experimental.pallas import tpu as pltpu
from jax.sharding import Mesh
from jax.sharding import PartitionSpec as P

AXES = ("y", "z", "l", "h", "c")
SIZES = {"y": 4, "z": 8, "l": 2, "h": 2, "c": 2}
ROWS = 88
SLOT = 96
QUART = 288
HALF = 576
WIDE = 640
CODED = 577
X = ("l", "h")
F32 = jnp.float32
BF16 = jnp.bfloat16
F16 = jnp.float16
VMEM = pl.BlockSpec(memory_space=pltpu.VMEM)
SMEM = pl.BlockSpec(memory_space=pltpu.SMEM)


def shape(dims, dtype):
    return jax.ShapeDtypeStruct(dims, dtype)


def call(kernel, outs, *args, smem=0, scratch=(), flops=0, mib=32):
    specs = [VMEM] * (len(args) - smem) + [SMEM] * smem
    moved = sum(a.size * a.dtype.itemsize for a in (*args, *outs))
    return pl.pallas_call(
        kernel,
        out_shape=outs,
        in_specs=specs,
        out_specs=[VMEM] * len(outs),
        scratch_shapes=list(scratch),
        compiler_params=pltpu.CompilerParams(vmem_limit_bytes=mib * 2**20),
        cost_estimate=pl.CostEstimate(flops=flops, bytes_accessed=moved, transcendentals=0),
    )(*args)


def flip(x, axis, mask):
    count = 4 if axis == X else SIZES[axis]
    return lax.ppermute(x, axis, [(i, i ^ mask) for i in range(count)])


def behind(x, axis, distance):
    count = SIZES[axis]
    return lax.ppermute(x, axis, [(i, (i + distance) % count) for i in range(count)])


def together(*xs):
    return lax.optimization_barrier(xs)


def split_kernel(image, text, image_keep, image_send, text_keep, text_send):
    for source, axis, keep, send in (
        (image, "h", image_keep, image_send),
        (text, "c", text_keep, text_send),
    ):
        low = lax.axis_index(axis) == 0
        x = source[...].astype(F32)
        first, second = x[:ROWS], x[ROWS:]
        keep[...] = jnp.where(low, first, second).astype(BF16)
        sent = jnp.where(low, second, first)
        if send is image_send:
            sent = jnp.concatenate([sent, jnp.zeros((ROWS, WIDE - QUART), F32)], axis=1)
            sent = jnp.concatenate([sent, jnp.zeros((SLOT - ROWS, WIDE), F32)], axis=0)
        send[...] = sent.astype(BF16)


def piece_kernel(keep, recv, out):
    a, b = keep[...].astype(F32), recv[...].astype(F32)[:ROWS, :QUART]
    out[...] = jnp.concatenate([a, b, jnp.zeros((ROWS, WIDE - HALF), F32)], axis=1).astype(BF16)


def stack_kernel(*refs):
    for n, ref in enumerate(refs[:-1]):
        refs[-1][n] = ref[...]


def scaled(x):
    most = jnp.max(jnp.max(jnp.abs(x), axis=0, keepdims=True), axis=1, keepdims=True)
    power = jnp.floor(jnp.log2(jnp.maximum(most, 1e-30)))
    lane = lax.broadcasted_iota(jnp.int32, x.shape, 1)
    return jnp.where(lane < HALF, x * jnp.exp2(13.0 - power), power)


def unscaled(p):
    return p * jnp.exp2(p[:1, HALF : HALF + 1] - 13.0)


def slope_kernel(*refs):
    halves, text, across = (refs[0:3], refs[3:6]), refs[6:9], refs[9]
    scale_ref, bias_ref = refs[10:12]
    send, slope, images, texts = refs[12:16]
    scale, bias = scale_ref[0], bias_ref[0]
    zeros = jnp.zeros((ROWS, WIDE - HALF), BF16)
    for s in range(8):
        rows = pl.ds(SLOT * s, ROWS)
        for half, parts in enumerate(halves):
            images[rows, WIDE * half : WIDE * (half + 1)] = parts[s // 3][s % 3]
        a, b = (text[0][s], across[s]) if s < 4 else (text[1][s - 4], text[2][s - 4])
        texts[rows, 0:WIDE] = jnp.concatenate([a[:, :QUART], b[:, :QUART], zeros], axis=1)
        texts[rows, WIDE:] = jnp.concatenate([a[:, QUART:HALF], b[:, QUART:HALF], zeros], axis=1)
        rows = pl.ds(SLOT * s + ROWS, SLOT - ROWS)
        images[rows, :] = jnp.zeros((SLOT - ROWS, 2 * WIDE), BF16)
        texts[rows, :] = jnp.zeros((SLOT - ROWS, 2 * WIDE), BF16)
    own = lax.axis_index("h") == lax.axis_index("c")
    for j in range(3):
        cols = pl.ds(256 * j, 256)
        dots = lax.dot_general(
            images[...], texts[cols, :], (((1,), (1,)), ((), ())), preferred_element_type=F32
        )
        logit = scale * dots + bias
        value = jax.nn.sigmoid(logit)
        if j == 0:
            top = logit[:SLOT]
            row = lax.broadcasted_iota(jnp.int32, top.shape, 0)
            col = lax.broadcasted_iota(jnp.int32, top.shape, 1)
            paired = (col == row) & (row < ROWS) & own
            top = jnp.where(paired, -jax.nn.sigmoid(-top), value[:SLOT])
            value = jnp.concatenate([top, value[SLOT:]], axis=0)
        slope[:, cols] = value.astype(BF16)
    image_terms(slope, texts, 1, send)


def image_terms(slope, texts, half, out):
    add = jnp.dot(slope[...], texts[:, WIDE * half : WIDE * (half + 1)], preferred_element_type=F32)
    for s in range(8):
        out[s] = add[SLOT * s : SLOT * s + ROWS, :]


def text_kernel(slope, images, texts, keep, own, two, three, *across):
    image_terms(slope, texts, 0, keep)
    total = lax.dot_general(
        slope[...], images[...], (((0,), (0,)), ((), ())), preferred_element_type=F32
    )
    pad = jnp.zeros((ROWS, CODED - HALF), F32)
    for s in range(8):
        x = total[SLOT * s : SLOT * s + ROWS, :]
        for d in range(2):
            low, high = x[:, QUART * d : QUART * (d + 1)], x[:, WIDE + QUART * d : WIDE + QUART * (d + 1)]
            part = jnp.concatenate([low, high, pad], axis=1)
            if s >= 4:
                (two, three)[d][s - 4] = scaled(part)
            elif d == 0:
                own[s] = part
            else:
                across[s][...] = part if s == 0 else scaled(part)


def image_first_kernel(keep, recv, own, below, above):
    for s in range(8):
        x = keep[s] + recv[s]
        if s < 3:
            own[s] = x
        else:
            (below, above)[s // 3 - 1][s % 3] = scaled(x)


def image_sum_kernel(own, from_above, from_below, kept, below, above):
    kept[...] = own[0] + unscaled(from_above[0]) + unscaled(from_below[0])
    below[...] = scaled(own[1] + unscaled(from_above[1]) + unscaled(from_below[1]))
    above[...] = scaled(own[2] + unscaled(from_above[2]))


def text_across_kernel(own, r1, r2, r3, out):
    out[...] = scaled(own[...] + unscaled(r1[...]) + unscaled(r2[...]) + unscaled(r3[...]))


def text_sum_kernel(own, r2, r3, kept, *outs):
    for n in range(4):
        x = own[n] + unscaled(r2[n]) + unscaled(r3[n])
        if n == 0:
            kept[...] = x
        else:
            outs[n - 1][...] = scaled(x)


def last_kernel(*refs):
    own, *parts, scale, keep, send = refs
    x = own[...]
    for part in parts:
        x = x + unscaled(part[...])
    x = scale[0] * x
    keep[...] = x[:, :QUART]
    send[:, :QUART] = x[:, QUART:HALF]
    if send.shape[1] > QUART:
        send[:, QUART:] = jnp.zeros((ROWS, send.shape[1] - QUART), F32)


def place_kernel(image_keep, image_recv, text_keep, text_recv, image_out, text_out):
    for axis, keep, recv, out in (
        ("h", image_keep, image_recv, image_out),
        ("c", text_keep, text_recv, text_out),
    ):
        low = lax.axis_index(axis) == 0
        a, b = keep[...], recv[...][:, :QUART]
        out[:ROWS] = jnp.where(low, a, b)
        out[ROWS:] = jnp.where(low, b, a)


def shards(image, text, scale, bias):
    scale, bias = scale.reshape(1), bias.reshape(1)
    half = shape((ROWS, QUART), BF16)
    image_keep, image_send, text_keep, text_send = call(
        split_kernel, [half, shape((SLOT, WIDE), BF16), half, half], image, text, mib=4
    )
    image_recv = flip(image_send, "h", 1)
    text_recv = flip(text_send, "c", 1)
    piece = [shape((ROWS, WIDE), BF16)]
    (text,) = call(piece_kernel, piece, text_keep, text_recv, mib=4)
    (image,) = call(piece_kernel, piece, image_keep, image_recv, mib=4)

    def stacked(*xs):
        return call(stack_kernel, [shape((len(xs), ROWS, WIDE), BF16)], *xs, mib=4)[0]

    four = stacked(text, *(flip(text, "y", n) for n in (1, 2, 3)))
    other = flip(text, "h", 1)
    other = [other] + [flip(other, "y", n) for n in (1, 2, 3)]
    texts = [four] + [flip(four, X, n) for n in (2, 3)]
    near = image, behind(image, "z", 3), behind(image, "z", -3)
    trio, duo, other = together(stacked(*near), stacked(*near[:2]), stacked(*other))
    images = [trio, behind(trio, "z", 1), behind(duo, "z", -1)]
    *images, t0, t1, t2 = together(*images, *texts)
    texts = [t0, t1, t2, other]
    swapped = [flip(x, "c", 1) for x in images]

    big, three, one = (shape((*d, ROWS, WIDE), F32) for d in ((8,), (3,), ()))
    quad, coded = shape((4, ROWS, CODED), F32), shape((ROWS, CODED), F32)
    two = shape((2, ROWS, WIDE), F32)
    joined = shape((8 * SLOT, 2 * WIDE), BF16)
    send, slope, images, texts = call(
        slope_kernel,
        [big, shape((8 * SLOT, 8 * SLOT), BF16), joined, joined],
        *images,
        *swapped,
        *texts,
        scale,
        bias,
        smem=2,
        flops=3 * 704 * 704 * 1152,
        mib=12,
    )
    recv = flip(send, "c", 1)
    keep, text_own, *text_out = call(
        text_kernel, [big] + [quad] * 3 + [coded] * 4, slope, images, texts, flops=3 * 704 * 704 * 1152, mib=12
    )
    text_out, text_across, *across_out = text_out[:2], *text_out[2:]
    image_own, below, above = call(image_first_kernel, [three, three, two], keep, recv, mib=12)
    below, above, *text_out = together(below, above, *text_out)

    def moved(x, move, axis, n):
        return move(x.astype(F16), axis, n).astype(F32)

    across_in = [moved(x, flip, "y", n) for n, x in enumerate(across_out, 1)]
    text_in = [moved(x, flip, X, n) for n, x in zip((2, 3), text_out)]
    image_in = [moved(below, behind, "z", -1), moved(above, behind, "z", 1)]
    (across,) = call(text_across_kernel, [coded], text_across, *across_in, mib=4)
    across = moved(across, flip, "h", 1)
    image_own, below, above = call(image_sum_kernel, [one] * 3, image_own, *image_in, mib=8)
    below, above = moved(below, behind, "z", -3), moved(above, behind, "z", 3)
    text_own, *text_out = call(text_sum_kernel, [coded] * 4, text_own, *text_in, mib=12)
    text_in = [across] + [moved(x, flip, "y", n) for n, x in enumerate(text_out, 1)]
    image_in = [below, above]
    part, wider = shape((ROWS, QUART), F32), shape((ROWS, 512), F32)
    image_keep, image_send = call(last_kernel, [part, wider], image_own, *image_in, scale, smem=1, mib=4)
    image_recv = flip(image_send, "h", 1)
    text_keep, text_send = call(last_kernel, [part, part], text_own, *text_in, scale, smem=1, mib=4)
    text_recv = flip(text_send, "c", 1)
    grads = [shape((2 * ROWS, QUART), F32)] * 2
    return tuple(call(place_kernel, grads, image_keep, image_recv, text_keep, text_recv, mib=4))


def solution(mesh):
    fine = Mesh(mesh.devices.reshape([SIZES[a] for a in AXES]), AXES)
    spec = P(("y", "z", "l"), ("h", "c"))
    return jax.shard_map(
        shards, mesh=fine, in_specs=(spec, spec, P(), P()), out_specs=(spec, spec), check_vma=False
    )
```

```python
import jax
import jax.numpy as jnp
from jax import lax
from jax.experimental import pallas as pl
from jax.experimental.pallas import tpu as pltpu
from jax.sharding import Mesh
from jax.sharding import PartitionSpec as P

AXES = ("y", "z", "l", "h", "c")
SIZES = {"y": 4, "z": 8, "l": 2, "h": 2, "c": 2}
ROWS = 88
SLOT = 96
QUART = 288
HALF = 576
WIDE = 640
CODED = 577
X = ("l", "h")
F32 = jnp.float32
BF16 = jnp.bfloat16
F16 = jnp.float16
VMEM = pl.BlockSpec(memory_space=pltpu.VMEM)
SMEM = pl.BlockSpec(memory_space=pltpu.SMEM)


def shape(dims, dtype):
    return jax.ShapeDtypeStruct(dims, dtype)


def call(kernel, outs, *args, smem=0, flops=0, mib=32):
    moved = sum(a.size * a.dtype.itemsize for a in (*args, *outs))
    return pl.pallas_call(
        kernel,
        out_shape=outs,
        in_specs=[VMEM] * (len(args) - smem) + [SMEM] * smem,
        out_specs=[VMEM] * len(outs),
        compiler_params=pltpu.CompilerParams(vmem_limit_bytes=mib * 2**20),
        cost_estimate=pl.CostEstimate(flops=flops, bytes_accessed=moved, transcendentals=0),
    )(*args)


def flip(x, axis, mask):
    count = 4 if axis == X else SIZES[axis]
    return lax.ppermute(x, axis, [(i, i ^ mask) for i in range(count)])


def behind(x, axis, distance):
    count = SIZES[axis]
    return lax.ppermute(x, axis, [(i, (i + distance) % count) for i in range(count)])


def together(*xs):
    return lax.optimization_barrier(xs)


def split_kernel(image, text, image_keep, image_send, text_keep, text_send):
    for source, axis, keep, send in (
        (image, "h", image_keep, image_send),
        (text, "c", text_keep, text_send),
    ):
        low = lax.axis_index(axis) == 0
        x = source[...].astype(F32)
        first, second = x[:ROWS], x[ROWS:]
        keep[...] = jnp.where(low, first, second).astype(BF16)
        sent = jnp.where(low, second, first)
        if send is image_send:
            sent = jnp.concatenate([sent, jnp.zeros((ROWS, WIDE - QUART), F32)], axis=1)
            sent = jnp.concatenate([sent, jnp.zeros((SLOT - ROWS, WIDE), F32)], axis=0)
        send[...] = sent.astype(BF16)


def piece_kernel(keep, recv, out):
    a, b = keep[...].astype(F32), recv[...].astype(F32)[:ROWS, :QUART]
    out[...] = jnp.concatenate([a, b, jnp.zeros((ROWS, WIDE - HALF), F32)], axis=1).astype(BF16)


def first_stack_kernel(text, r1, r2, r3, scale, bias, out, scalars):
    stack_kernel(text, r1, r2, r3, out)
    scalars[:8] = jnp.full((8, 128), scale[0])
    scalars[8:] = jnp.full((8, 128), bias[0])


def stack_kernel(*refs):
    for n, ref in enumerate(refs[:-1]):
        refs[-1][n] = ref[...]


def scaled(x):
    most = jnp.max(jnp.max(jnp.abs(x), axis=0, keepdims=True), axis=1, keepdims=True)
    power = jnp.floor(jnp.log2(jnp.maximum(most, 1e-30)))
    lane = lax.broadcasted_iota(jnp.int32, x.shape, 1)
    return jnp.where(lane < HALF, x * jnp.exp2(13.0 - power), power)


def unscaled(p):
    return p * jnp.exp2(p[:1, HALF : HALF + 1] - 13.0)


def near_kernel(image, swapped, four, two, three, across, scalars, send, slope, images, texts):
    zeros = jnp.zeros((ROWS, WIDE - HALF), BF16)
    for s in range(8):
        rows = pl.ds(SLOT * s, ROWS)
        a, b = (four[s], across[s]) if s < 4 else (two[s - 4], three[s - 4])
        texts[rows, 0:WIDE] = jnp.concatenate([a[:, :QUART], b[:, :QUART], zeros], axis=1)
        texts[rows, WIDE:] = jnp.concatenate([a[:, QUART:HALF], b[:, QUART:HALF], zeros], axis=1)
        texts[pl.ds(SLOT * s + ROWS, SLOT - ROWS), :] = jnp.zeros((SLOT - ROWS, 2 * WIDE), BF16)
    join_images(images, ((image, swapped),))
    own = lax.axis_index("h") == lax.axis_index("c")
    slopes(scalars, slope, images, texts, own)
    image_terms(slope, texts, 1, send)


def far_kernel(below, below_swapped, above, above_swapped, texts, scalars, send, slope, images):
    join_images(images, ((below, below_swapped), (above, above_swapped)))
    slopes(scalars, slope, images, texts, None)
    image_terms(slope, texts, 1, send)


def join_images(images, parts):
    s = 0
    for part, swapped in parts:
        for n in range(part.shape[0]):
            images[pl.ds(SLOT * s, ROWS), 0:WIDE] = part[n]
            images[pl.ds(SLOT * s, ROWS), WIDE:] = swapped[n]
            images[pl.ds(SLOT * s + ROWS, SLOT - ROWS), :] = jnp.zeros((SLOT - ROWS, 2 * WIDE), BF16)
            s += 1


def slopes(scalars, slope, images, texts, own):
    scale, bias = scalars[0:1, 0:1], scalars[8:9, 0:1]
    for j in range(3):
        cols = pl.ds(256 * j, 256)
        dots = lax.dot_general(
            images[...], texts[cols, :], (((1,), (1,)), ((), ())), preferred_element_type=F32
        )
        logit = scale * dots + bias
        value = jax.nn.sigmoid(logit)
        if j == 0 and own is not None:
            top = logit[:SLOT]
            row = lax.broadcasted_iota(jnp.int32, top.shape, 0)
            col = lax.broadcasted_iota(jnp.int32, top.shape, 1)
            paired = (col == row) & (row < ROWS) & own
            top = jnp.where(paired, -jax.nn.sigmoid(-top), value[:SLOT])
            value = jnp.concatenate([top, value[SLOT:]], axis=0)
        slope[:, cols] = value.astype(BF16)


def image_terms(slope, texts, half, out):
    add = jnp.dot(slope[...], texts[:, WIDE * half : WIDE * (half + 1)], preferred_element_type=F32)
    for s in range(out.shape[0]):
        out[s] = add[SLOT * s : SLOT * s + ROWS, :]


def text_kernel(slope, images, far_slope, far_images, texts, keep, far_keep, own, two, three, *across):
    image_terms(far_slope, texts, 0, far_keep)
    image_terms(slope, texts, 0, keep)
    total = lax.dot_general(
        slope[...], images[...], (((0,), (0,)), ((), ())), preferred_element_type=F32
    ) + lax.dot_general(
        far_slope[...], far_images[...], (((0,), (0,)), ((), ())), preferred_element_type=F32
    )
    pad = jnp.zeros((ROWS, CODED - HALF), F32)
    for s in range(8):
        x = total[SLOT * s : SLOT * s + ROWS, :]
        for d in range(2):
            low, high = x[:, QUART * d : QUART * (d + 1)], x[:, WIDE + QUART * d : WIDE + QUART * (d + 1)]
            part = jnp.concatenate([low, high, pad], axis=1)
            if s >= 4:
                (two, three)[d][s - 4] = scaled(part)
            elif d == 0:
                own[s] = part
            else:
                across[s][...] = part if s == 0 else scaled(part)


def image_first_kernel(keep, recv, far_keep, far_recv, own, below, above):
    for s in range(5):
        (below, above)[s // 3][s % 3] = scaled(far_keep[s] + far_recv[s])
    for s in range(3):
        own[s] = keep[s] + recv[s]


def image_sum_kernel(own, from_above, from_below, kept, below, above):
    kept[...] = own[0] + unscaled(from_above[0]) + unscaled(from_below[0])
    below[...] = scaled(own[1] + unscaled(from_above[1]) + unscaled(from_below[1]))
    above[...] = scaled(own[2] + unscaled(from_above[2]))


def text_across_kernel(own, r1, r2, r3, out):
    out[...] = scaled(own[...] + unscaled(r1[...]) + unscaled(r2[...]) + unscaled(r3[...]))


def text_sum_kernel(own, r2, r3, kept, *outs):
    for n in range(4):
        x = own[n] + unscaled(r2[n]) + unscaled(r3[n])
        if n == 0:
            kept[...] = x
        else:
            outs[n - 1][...] = scaled(x)


def last_kernel(*refs):
    own, *parts, scalars, keep, send = refs
    x = own[...]
    for part in parts:
        x = x + unscaled(part[...])
    x = scalars[0:1, 0:1] * x
    keep[...] = x[:, :QUART]
    send[:, :QUART] = x[:, QUART:HALF]
    if send.shape[1] > QUART:
        send[:, QUART:] = jnp.zeros((ROWS, send.shape[1] - QUART), F32)


def place_kernel(image_keep, image_recv, text_keep, text_recv, image_out, text_out):
    for axis, keep, recv, out in (
        ("h", image_keep, image_recv, image_out),
        ("c", text_keep, text_recv, text_out),
    ):
        low = lax.axis_index(axis) == 0
        a, b = keep[...], recv[...][:, :QUART]
        out[:ROWS] = jnp.where(low, a, b)
        out[ROWS:] = jnp.where(low, b, a)


def shards(image, text, scale, bias):
    half = shape((ROWS, QUART), BF16)
    image_keep, image_send, text_keep, text_send = call(
        split_kernel, [half, shape((SLOT, WIDE), BF16), half, half], image, text, mib=4
    )
    image_recv = flip(image_send, "h", 1)
    text_recv = flip(text_send, "c", 1)
    piece = [shape((ROWS, WIDE), BF16)]
    (text,) = call(piece_kernel, piece, text_keep, text_recv, mib=4)
    (image,) = call(piece_kernel, piece, image_keep, image_recv, mib=4)

    def stacked(*xs):
        return call(stack_kernel, [shape((len(xs), ROWS, WIDE), BF16)], *xs, mib=4)[0]

    four, scalars = call(
        first_stack_kernel,
        [shape((4, ROWS, WIDE), BF16), shape((16, 128), F32)],
        text,
        *(flip(text, "y", n) for n in (1, 2, 3)),
        scale.reshape(1),
        bias.reshape(1),
        smem=2,
        mib=4,
    )
    other = flip(text, "h", 1)
    other = [other] + [flip(other, "y", n) for n in (1, 2, 3)]
    texts = [four] + [flip(four, X, n) for n in (2, 3)]
    near = image, behind(image, "z", 3), behind(image, "z", -3)
    trio, duo, other = together(stacked(*near), stacked(*near[:2]), stacked(*other))
    images = [trio, behind(trio, "z", 1), behind(duo, "z", -1)]
    *images, four, two_x, three_x = together(*images, *texts)
    swapped = [flip(x, "c", 1) for x in (trio, *images[1:])]

    three, five, one = (shape((*d, ROWS, WIDE), F32) for d in ((3,), (5,), ()))
    two = shape((2, ROWS, WIDE), F32)
    quad, coded = shape((4, ROWS, CODED), F32), shape((ROWS, CODED), F32)

    def joined(n, lanes):
        return shape((n * SLOT, lanes), BF16)

    flops = 2 * 704 * 704 * 1152
    send, slope, images_near, texts = call(
        near_kernel,
        [three, joined(3, 8 * SLOT), joined(3, 2 * WIDE), joined(8, 2 * WIDE)],
        trio,
        swapped[0],
        four,
        two_x,
        three_x,
        other,
        scalars,
        flops=flops // 2,
        mib=12,
    )
    recv = flip(send, "c", 1)
    send, far_slope, far_images = call(
        far_kernel,
        [five, joined(5, 8 * SLOT), joined(5, 2 * WIDE)],
        images[1],
        swapped[1],
        images[2],
        swapped[2],
        texts,
        scalars,
        flops=flops,
        mib=12,
    )
    far_recv = flip(send, "c", 1)
    keep, far_keep, text_own, *text_out = call(
        text_kernel,
        [three, five] + [quad] * 3 + [coded] * 4,
        slope,
        images_near,
        far_slope,
        far_images,
        texts,
        flops=3 * flops // 2,
        mib=12,
    )
    text_out, text_across, *across_out = text_out[:2], *text_out[2:]
    image_own, below, above = call(
        image_first_kernel, [three, three, two], keep, recv, far_keep, far_recv, mib=12
    )
    below, above, *text_out = together(below, above, *text_out)

    def moved(x, move, axis, n):
        return move(x.astype(F16), axis, n).astype(F32)

    across_in = [moved(x, flip, "y", n) for n, x in enumerate(across_out, 1)]
    text_in = [moved(x, flip, X, n) for n, x in zip((2, 3), text_out)]
    image_in = [moved(below, behind, "z", -1), moved(above, behind, "z", 1)]
    (across,) = call(text_across_kernel, [coded], text_across, *across_in, mib=4)
    across = moved(across, flip, "h", 1)
    image_own, below, above = call(image_sum_kernel, [one] * 3, image_own, *image_in, mib=8)
    below, above = moved(below, behind, "z", -3), moved(above, behind, "z", 3)
    text_own, *text_out = call(text_sum_kernel, [coded] * 4, text_own, *text_in, mib=12)
    text_in = [across] + [moved(x, flip, "y", n) for n, x in enumerate(text_out, 1)]
    image_in = [below, above]
    part, wider = shape((ROWS, QUART), F32), shape((ROWS, 512), F32)
    image_keep, image_send = call(last_kernel, [part, wider], image_own, *image_in, scalars, mib=4)
    image_recv = flip(image_send, "h", 1)
    text_keep, text_send = call(last_kernel, [part, part], text_own, *text_in, scalars, mib=4)
    text_recv = flip(text_send, "c", 1)
    grads = [shape((2 * ROWS, QUART), F32)] * 2
    return tuple(call(place_kernel, grads, image_keep, image_recv, text_keep, text_recv, mib=4))


def solution(mesh):
    fine = Mesh(mesh.devices.reshape([SIZES[a] for a in AXES]), AXES)
    spec = P(("y", "z", "l"), ("h", "c"))
    return jax.shard_map(
        shards, mesh=fine, in_specs=(spec, spec, P(), P()), out_specs=(spec, spec), check_vma=False
    )
```

```python
import jax
import jax.numpy as jnp
from jax import lax
from jax.experimental import pallas as pl
from jax.experimental.pallas import tpu as pltpu
from jax.sharding import Mesh
from jax.sharding import PartitionSpec as P

AXES = ("y", "z", "l", "h", "c")
SIZES = {"y": 4, "z": 8, "l": 2, "h": 2, "c": 2}
ROWS = 88
SLOT = 96
QUART = 288
HALF = 576
WIDE = 640
CODED = 577
X = ("l", "h")
F32 = jnp.float32
BF16 = jnp.bfloat16
F16 = jnp.float16
VMEM = pl.BlockSpec(memory_space=pltpu.VMEM)
SMEM = pl.BlockSpec(memory_space=pltpu.SMEM)


def shape(dims, dtype):
    return jax.ShapeDtypeStruct(dims, dtype)


def call(kernel, outs, *args, smem=0, flops=0, mib=32):
    moved = sum(a.size * a.dtype.itemsize for a in (*args, *outs))
    return pl.pallas_call(
        kernel,
        out_shape=outs,
        in_specs=[VMEM] * (len(args) - smem) + [SMEM] * smem,
        out_specs=[VMEM] * len(outs),
        compiler_params=pltpu.CompilerParams(vmem_limit_bytes=mib * 2**20),
        cost_estimate=pl.CostEstimate(flops=flops, bytes_accessed=moved, transcendentals=0),
    )(*args)


def flip(x, axis, mask):
    count = 4 if axis == X else SIZES[axis]
    return lax.ppermute(x, axis, [(i, i ^ mask) for i in range(count)])


def behind(x, axis, distance):
    count = SIZES[axis]
    return lax.ppermute(x, axis, [(i, (i + distance) % count) for i in range(count)])


def together(*xs):
    return lax.optimization_barrier(xs)


def split_kernel(image, text, image_keep, image_send, text_keep, text_send):
    for source, axis, keep, send in (
        (image, "h", image_keep, image_send),
        (text, "c", text_keep, text_send),
    ):
        low = lax.axis_index(axis) == 0
        x = source[...].astype(F32)
        first, second = x[:ROWS], x[ROWS:]
        keep[...] = jnp.where(low, first, second).astype(BF16)
        sent = jnp.where(low, second, first)
        if send is image_send:
            sent = jnp.concatenate([sent, jnp.zeros((ROWS, WIDE - QUART), F32)], axis=1)
        send[...] = sent.astype(BF16)


def piece_kernel(keep, recv, out):
    a, b = keep[...].astype(F32), recv[...].astype(F32)[:ROWS, :QUART]
    out[...] = jnp.concatenate([a, b, jnp.zeros((ROWS, WIDE - HALF), F32)], axis=1).astype(BF16)


def first_stack_kernel(text, r1, r2, r3, scale, bias, out, scalars):
    stack_kernel(text, r1, r2, r3, out)
    scalars[:8] = jnp.full((8, 128), scale[0])
    scalars[8:] = jnp.full((8, 128), bias[0])


def stack_kernel(*refs):
    for n, ref in enumerate(refs[:-1]):
        refs[-1][n] = ref[...]


def scaled(x):
    most = jnp.max(jnp.max(jnp.abs(x), axis=0, keepdims=True), axis=1, keepdims=True)
    power = jnp.floor(jnp.log2(jnp.maximum(most, 1e-30)))
    lane = lax.broadcasted_iota(jnp.int32, x.shape, 1)
    return jnp.where(lane < HALF, x * jnp.exp2(13.0 - power), power)


def unscaled(p):
    return p * jnp.exp2(p[:1, HALF : HALF + 1] - 13.0)


def near_kernel(image, swapped, four, two, three, across, scalars, send, slope, images, texts):
    zeros = jnp.zeros((ROWS, WIDE - HALF), BF16)
    for s in range(8):
        rows = pl.ds(SLOT * s, ROWS)
        a, b = (four[s], across[s]) if s < 4 else (two[s - 4], three[s - 4])
        texts[rows, 0:WIDE] = jnp.concatenate([a[:, :QUART], b[:, :QUART], zeros], axis=1)
        texts[rows, WIDE:] = jnp.concatenate([a[:, QUART:HALF], b[:, QUART:HALF], zeros], axis=1)
        texts[pl.ds(SLOT * s + ROWS, SLOT - ROWS), :] = jnp.zeros((SLOT - ROWS, 2 * WIDE), BF16)
    join_images(images, ((image, swapped),))
    own = lax.axis_index("h") == lax.axis_index("c")
    slopes(scalars, slope, images, texts, own)
    image_terms(slope, texts, 1, send)


def far_kernel(below, below_swapped, above, above_swapped, texts, scalars, send, slope, images):
    join_images(images, ((below, below_swapped), (above, above_swapped)))
    slopes(scalars, slope, images, texts, None)
    image_terms(slope, texts, 1, send)


def join_images(images, parts):
    s = 0
    for part, swapped in parts:
        for n in range(part.shape[0]):
            images[pl.ds(SLOT * s, ROWS), 0:WIDE] = part[n]
            images[pl.ds(SLOT * s, ROWS), WIDE:] = swapped[n]
            images[pl.ds(SLOT * s + ROWS, SLOT - ROWS), :] = jnp.zeros((SLOT - ROWS, 2 * WIDE), BF16)
            s += 1


def slopes(scalars, slope, images, texts, own):
    scale, bias = scalars[0:1, 0:1], scalars[8:9, 0:1]
    for j in range(3):
        cols = pl.ds(256 * j, 256)
        dots = lax.dot_general(
            images[...], texts[cols, :], (((1,), (1,)), ((), ())), preferred_element_type=F32
        )
        logit = scale * dots + bias
        value = jax.nn.sigmoid(logit)
        if j == 0 and own is not None:
            top = logit[:SLOT]
            row = lax.broadcasted_iota(jnp.int32, top.shape, 0)
            col = lax.broadcasted_iota(jnp.int32, top.shape, 1)
            paired = (col == row) & (row < ROWS) & own
            top = jnp.where(paired, -jax.nn.sigmoid(-top), value[:SLOT])
            value = jnp.concatenate([top, value[SLOT:]], axis=0)
        slope[:, cols] = value.astype(BF16)


def image_terms(slope, texts, half, out):
    add = jnp.dot(slope[...], texts[:, WIDE * half : WIDE * (half + 1)], preferred_element_type=F32)
    for s in range(out.shape[0]):
        out[s] = add[SLOT * s : SLOT * s + ROWS, :]


def text_kernel(slope, images, far_slope, far_images, texts, keep, far_keep, own, two, three, *across):
    image_terms(far_slope, texts, 0, far_keep)
    image_terms(slope, texts, 0, keep)
    total = lax.dot_general(
        slope[...], images[...], (((0,), (0,)), ((), ())), preferred_element_type=F32
    ) + lax.dot_general(
        far_slope[...], far_images[...], (((0,), (0,)), ((), ())), preferred_element_type=F32
    )
    pad = jnp.zeros((ROWS, CODED - HALF), F32)
    for s in range(8):
        x = total[SLOT * s : SLOT * s + ROWS, :]
        for d in range(2):
            low, high = x[:, QUART * d : QUART * (d + 1)], x[:, WIDE + QUART * d : WIDE + QUART * (d + 1)]
            part = jnp.concatenate([low, high, pad], axis=1)
            if s >= 4:
                (two, three)[d][s - 4] = scaled(part)
            elif d == 0:
                own[s] = part
            else:
                across[s][...] = part if s == 0 else scaled(part)


def image_first_kernel(keep, recv, far_keep, far_recv, own, below, above):
    for s in range(5):
        (below, above)[s // 3][s % 3] = scaled(far_keep[s] + far_recv[s])
    for s in range(3):
        own[s] = keep[s] + recv[s]


def image_sum_kernel(own, from_above, from_below, kept, below, above):
    kept[...] = own[0] + unscaled(from_above[0]) + unscaled(from_below[0])
    below[...] = scaled(own[1] + unscaled(from_above[1]) + unscaled(from_below[1]))
    above[...] = scaled(own[2] + unscaled(from_above[2]))


def text_across_kernel(own, r1, r2, r3, out):
    out[...] = scaled(own[...] + unscaled(r1[...]) + unscaled(r2[...]) + unscaled(r3[...]))


def text_sum_kernel(own, r2, r3, kept, *outs):
    for n in range(4):
        x = own[n] + unscaled(r2[n]) + unscaled(r3[n])
        if n == 0:
            kept[...] = x
        else:
            outs[n - 1][...] = scaled(x)


def last_kernel(*refs):
    own, *parts, scalars, keep, send = refs
    x = own[...]
    for part in parts:
        x = x + unscaled(part[...])
    x = scalars[0:1, 0:1] * x
    keep[...] = x[:, :QUART]
    send[:, :QUART] = x[:, QUART:HALF]
    if send.shape[1] > QUART:
        send[:, QUART:] = jnp.zeros((ROWS, send.shape[1] - QUART), F32)


def place_kernel(image_keep, image_recv, text_keep, text_recv, image_out, text_out):
    for axis, keep, recv, out in (
        ("h", image_keep, image_recv, image_out),
        ("c", text_keep, text_recv, text_out),
    ):
        low = lax.axis_index(axis) == 0
        a, b = keep[...], recv[...][:, :QUART]
        out[:ROWS] = jnp.where(low, a, b)
        out[ROWS:] = jnp.where(low, b, a)


def shards(image, text, scale, bias):
    half = shape((ROWS, QUART), BF16)
    image_keep, image_send, text_keep, text_send = call(
        split_kernel, [half, shape((ROWS, WIDE), BF16), half, half], image, text, mib=4
    )
    image_recv = flip(image_send, "h", 1)
    text_recv = flip(text_send, "c", 1)
    piece = [shape((ROWS, WIDE), BF16)]
    (text,) = call(piece_kernel, piece, text_keep, text_recv, mib=4)
    (image,) = call(piece_kernel, piece, image_keep, image_recv, mib=4)

    def stacked(*xs):
        return call(stack_kernel, [shape((len(xs), ROWS, WIDE), BF16)], *xs, mib=4)[0]

    four, scalars = call(
        first_stack_kernel,
        [shape((4, ROWS, WIDE), BF16), shape((16, 128), F32)],
        text,
        *(flip(text, "y", n) for n in (1, 2, 3)),
        scale.reshape(1),
        bias.reshape(1),
        smem=2,
        mib=4,
    )
    other = flip(text, "h", 1)
    other = [other] + [flip(other, "y", n) for n in (1, 2, 3)]
    texts = [four] + [flip(four, X, n) for n in (2, 3)]
    near = image, behind(image, "z", 3), behind(image, "z", -3)
    trio, duo, other = together(stacked(*near), stacked(*near[:2]), stacked(*other))
    images = [trio, behind(trio, "z", 1), behind(duo, "z", -1)]
    *images, four, two_x, three_x = together(*images, *texts)
    swapped = [flip(x, "c", 1) for x in (trio, *images[1:])]

    three, five, one = (shape((*d, ROWS, WIDE), F32) for d in ((3,), (5,), ()))
    two = shape((2, ROWS, WIDE), F32)
    quad, coded = shape((4, ROWS, CODED), F32), shape((ROWS, CODED), F32)

    def joined(n, lanes):
        return shape((n * SLOT, lanes), BF16)

    flops = 2 * 704 * 704 * 1152
    send, slope, images_near, texts = call(
        near_kernel,
        [three, joined(3, 8 * SLOT), joined(3, 2 * WIDE), joined(8, 2 * WIDE)],
        trio,
        swapped[0],
        four,
        two_x,
        three_x,
        other,
        scalars,
        flops=flops // 2,
        mib=12,
    )
    recv = flip(send, "c", 1)
    send, far_slope, far_images = call(
        far_kernel,
        [five, joined(5, 8 * SLOT), joined(5, 2 * WIDE)],
        images[1],
        swapped[1],
        images[2],
        swapped[2],
        texts,
        scalars,
        flops=flops,
        mib=12,
    )
    far_recv = flip(send, "c", 1)
    keep, far_keep, text_own, *text_out = call(
        text_kernel,
        [three, five] + [quad] * 3 + [coded] * 4,
        slope,
        images_near,
        far_slope,
        far_images,
        texts,
        flops=3 * flops // 2,
        mib=12,
    )
    text_out, text_across, *across_out = text_out[:2], *text_out[2:]
    image_own, below, above = call(
        image_first_kernel, [three, three, two], keep, recv, far_keep, far_recv, mib=12
    )

    def moved(x, move, axis, n):
        return move(x.astype(F16), axis, n).astype(F32)

    across_in = [moved(x, flip, "y", n) for n, x in enumerate(across_out, 1)]
    text_in = [moved(x, flip, X, n) for n, x in zip((2, 3), text_out)]
    image_in = [moved(below, behind, "z", -1), moved(above, behind, "z", 1)]
    (across,) = call(text_across_kernel, [coded], text_across, *across_in, mib=4)
    across = moved(across, flip, "h", 1)
    image_own, below, above = call(image_sum_kernel, [one] * 3, image_own, *image_in, mib=8)
    below, above = moved(below, behind, "z", -3), moved(above, behind, "z", 3)
    text_own, *text_out = call(text_sum_kernel, [coded] * 4, text_own, *text_in, mib=12)
    text_in = [across] + [moved(x, flip, "y", n) for n, x in enumerate(text_out, 1)]
    image_in = [below, above]
    part, wider = shape((ROWS, QUART), F32), shape((ROWS, 512), F32)
    image_keep, image_send = call(last_kernel, [part, wider], image_own, *image_in, scalars, mib=4)
    image_recv = flip(image_send, "h", 1)
    text_keep, text_send = call(last_kernel, [part, part], text_own, *text_in, scalars, mib=4)
    text_recv = flip(text_send, "c", 1)
    grads = [shape((2 * ROWS, QUART), F32)] * 2
    return tuple(call(place_kernel, grads, image_keep, image_recv, text_keep, text_recv, mib=4))


def solution(mesh):
    fine = Mesh(mesh.devices.reshape([SIZES[a] for a in AXES]), AXES)
    spec = P(("y", "z", "l"), ("h", "c"))
    return jax.shard_map(
        shards, mesh=fine, in_specs=(spec, spec, P(), P()), out_specs=(spec, spec), check_vma=False
    )
```
